256 devices in a mesh: chan: 8 (over x, y_hi), seg: 32 (over y_lo, z, core).
Axes of the slice: x: 4, y: 4 (y_hi: 2, y_lo: 2; y = y_hi * 2 + y_lo), z: 8, core: 2. Of those that a mesh axis runs over, the one named last changes fastest.
Arguments:
- spectra: bfloat16 [128, 2, 200, 1024], P('seg', None, None, 'chan'), may hold values from -6 to 6
- match: int32 [3, 8], replicated, may hold values from 0 to 7, as said below
- counts: int32 [32], P('seg'), may hold values from 1 to 4, as said below
Outputs:
- correlations: float32 [3, 51, 1024, 128], P(None, None, ('chan', 'seg'))
The draws below stay inside these ranges and needn't reach their ends.
Inputs may be any that keep to these rules, and one draw needn't show every extreme that they name: In each round partnership is mutual (match[r, match[r, c]] = c); a block may be its own partner; rounds are drawn independently and may repeat. `counts`: some group has all 4 slots valid.
All inputs are finite; a program needn't handle non-finite values.
Results may differ from the reference program's by a relative error of at most 0.0003.
Values may be sent and summed in bfloat16 or wider, within the bound.
No kernel may reach another device: no remote copies, remote signals or barrier semaphores. Data moves between devices by JAX's collectives and lax.ppermute only.
A program may use at most 128 MiB of HBM per device.

```python
import jax
import jax.numpy as jnp
from jax import lax

CH_DEV = 128
FREQ = 200
LAGS = 51
SAMPLES = 3000
ROUNDS = 3
SEG_CAP = 4
CHANNELS = 1024
SEGMENTS = 128
N_CHAN = 8
N_SEG = 32


def slot_team(slot, turn):
    return jnp.where(slot == 0, 0, (slot - 1 + turn) % (N_CHAN - 1) + 1)


def draw_match(key, part):
    key = jax.random.fold_in(key, 1)
    key_labels, key_rounds, key_split = jax.random.split(key, 3)
    labels = jax.random.permutation(key_labels, N_CHAN).astype(jnp.int32)
    turns = jax.random.randint(key_rounds, (ROUNDS, 1), 0, N_CHAN - 1).astype(jnp.int32)
    slots = jnp.arange(N_CHAN, dtype=jnp.int32)[None, :]
    team = slot_team(slots, turns)
    rival = slot_team(N_CHAN - 1 - slots, turns)
    pair_index = jnp.minimum(slots, N_CHAN - 1 - slots) + jnp.zeros_like(turns)
    split_bits = jax.random.randint(key_split, (ROUNDS, N_CHAN // 2), 0, 4).astype(jnp.int32)
    split_pair = jnp.take_along_axis(split_bits, pair_index, axis=1) == 0
    partner = jnp.where(split_pair, labels[team], labels[rival])
    rows = jnp.arange(ROUNDS, dtype=jnp.int32)[:, None] + jnp.zeros_like(slots)
    table = jnp.zeros((ROUNDS, N_CHAN), jnp.int32)
    return table.at[rows, labels[team]].set(partner)


def draw_counts(key, part):
    key = jax.random.fold_in(key, 2)
    key_values, key_place = jax.random.split(key)
    values = jax.random.randint(key_values, (N_SEG,), 1, SEG_CAP + 1).astype(jnp.int32)
    place = jax.random.randint(key_place, (), 0, N_SEG)
    return values.at[place].set(SEG_CAP)


def level_of(key, extent, shards, low, largest):
    def one(dim, shards_of):
        heights = jax.random.uniform(jax.random.fold_in(jax.random.fold_in(key, 6), dim), (shards_of,), jnp.float32, low / len(shards), largest / len(shards))
        return jnp.repeat(jnp.exp(heights), extent[dim] // shards_of).reshape((-1,) + (1,) * (len(extent) - dim - 1))

    loudness = one(*shards[0])
    for cut in shards[1:]:
        loudness = loudness * one(*cut)
    return loudness


def noise(stream_key, extent, width, limit, cuts=(), held_as=jnp.bfloat16):
    values = width * jax.random.normal(stream_key, extent, jnp.float32)
    if cuts:
        values = values * level_of(stream_key, extent, cuts, -0.22, 0.18)
    return jnp.clip(values, -limit, limit).astype(held_as)


def setup_inputs(seed: int = 0) -> dict:
    arg_keys = jax.random.split(jax.random.key(seed), 4)
    spectra = noise(arg_keys[0], (SEGMENTS, 2, FREQ, CHANNELS), 1.0, 6.0, ((0, 32), (3, 8)))
    match = draw_match(jax.random.fold_in(arg_keys[3], 71), 0)
    counts = draw_counts(jax.random.fold_in(arg_keys[3], 71), 0)
    return dict(spectra=spectra, match=match, counts=counts)


def lag_table():
    lag = jnp.arange(LAGS, dtype=jnp.float32)[:, None] - jnp.float32(LAGS // 2)
    freq = jnp.arange(FREQ, dtype=jnp.float32)[None, :] + 1.0
    angle = 2.0 * jnp.pi * freq * lag / jnp.float32(SAMPLES)
    return jnp.concatenate([jnp.cos(angle), -jnp.sin(angle)], axis=1)

def reference(spectra, match, counts):
    slots = jnp.arange(SEGMENTS, dtype=jnp.int32)
    valid = (slots % SEG_CAP < counts[slots // SEG_CAP]).astype(jnp.float32)
    total = jnp.sum(counts).astype(jnp.float32)
    table = lag_table()

    def one_round(r):

        def one_block(c):
            partner = match[r, c]
            own = lax.dynamic_slice_in_dim(spectra, (c * CH_DEV).astype(jnp.int32), CH_DEV, 3).astype(jnp.float32)
            own = own * valid[:, None, None, None]
            other = lax.dynamic_slice_in_dim(spectra, (partner * CH_DEV).astype(jnp.int32), CH_DEV, 3).astype(jnp.float32)
            rotated = jnp.stack([-other[:, 1], other[:, 0]], axis=1)
            real = jnp.einsum('spfa,spfb->fab', own, other, precision=lax.Precision.HIGHEST)
            imag = jnp.einsum('spfa,spfb->fab', own, rotated, precision=lax.Precision.HIGHEST)
            both = jnp.concatenate([real, imag], axis=0).reshape(2 * FREQ, CH_DEV * CH_DEV)
            lagged = jnp.dot(table, both, precision=lax.Precision.HIGHEST)
            return lagged.reshape(LAGS, CH_DEV, CH_DEV)
        blocks = lax.map(one_block, jnp.arange(N_CHAN, dtype=jnp.int32))
        return jnp.transpose(blocks, (1, 0, 2, 3)).reshape(LAGS, CHANNELS, CH_DEV)
    result = jnp.stack([one_round(r) for r in range(ROUNDS)], axis=0)
    return result / jnp.sqrt(total * jnp.float32(FREQ))
```

```python
import jax
import jax.numpy as jnp
import numpy as np
from jax import lax
from jax.experimental import pallas as pl
from jax.experimental.pallas import tpu as pltpu
from jax.sharding import PartitionSpec as P

LAGS = 51
SAMPLES = 3000
ROUNDS = 3
HALF = LAGS // 2
ROWS = 32


def tables(freq, bins):
    lag = np.arange(ROWS, dtype=np.float64)[:, None]
    f = np.arange(bins, dtype=np.float64)[None, :] + 1.0
    angle = 2.0 * np.pi * f * lag / SAMPLES
    live = (np.arange(bins)[None, :] < freq) & (np.arange(ROWS)[:, None] <= HALF)
    return (
        np.where(live, np.cos(angle), 0.0).astype(np.float32),
        np.where(live, np.sin(angle), 0.0).astype(np.float32),
    )


def cross_kernel(match, x, out, turned):
    blocks, depth, block = x.shape
    tile = 2 * (block // 32)
    sources = depth // tile

    row = lax.broadcasted_iota(jnp.int32, (2 * block, 2 * block), 0)
    col = lax.broadcasted_iota(jnp.int32, (2 * block, 2 * block), 1)
    half = tile // 2
    channel = (row // tile) * half + row % half
    part = (row % tile) // half
    order = (col == part * block + channel).astype(jnp.bfloat16)

    def turn(c, _):
        own = x[c]
        groups = own.astype(jnp.float32).reshape(sources, tile, block)
        swapped = jnp.concatenate([groups[:, half:], -groups[:, :half]], axis=1)
        both = jnp.concatenate([own, swapped.reshape(depth, block).astype(jnp.bfloat16)], axis=1)
        turned[c] = lax.dot_general(
            order, both, (((1,), (1,)), ((), ())), preferred_element_type=jnp.float32
        ).astype(jnp.bfloat16)
        return 0

    lax.fori_loop(0, blocks, turn, 0)

    def one(c, _):
        for r in range(ROUNDS):
            product = jnp.dot(turned[c], x[match[r, c]], preferred_element_type=jnp.float32)
            out[pl.ds(c * 32, 32), r * tile : (r + 1) * tile, :] = product.reshape(32, tile, block)
        return 0

    lax.fori_loop(0, blocks, one, 0)


def split(v):
    high = v.astype(jnp.bfloat16)
    return high, (v - high.astype(jnp.float32)).astype(jnp.bfloat16)


def lag_kernel(freq, cos, sin, x, out):
    bins = cos.shape[1]
    rows = x.shape[0] // bins
    tile = rows // ROUNDS
    half = tile // 2
    cos_high, cos_low = split(cos[...])
    sin_high, sin_low = split(sin[...])
    cos_both = jnp.concatenate([cos_high, cos_low], axis=0)
    sin_both = jnp.concatenate([sin_high, sin_low], axis=0)

    def apply(both, top, v):
        high, low = split(v)
        first = jnp.dot(both, high, preferred_element_type=jnp.float32)
        return first[:ROWS] + first[ROWS:] + jnp.dot(top, low, preferred_element_type=jnp.float32)

    for r in range(ROUNDS):
        for a in range(half):
            at = r * tile + a
            real = x[pl.ds(at, bins, stride=rows), :]
            imag = x[pl.ds(at + half, bins, stride=rows), :]
            total = real[freq : freq + 1, :]
            scale = lax.rsqrt(total * jnp.float32(freq))
            even = apply(cos_both, cos_high, real) * scale
            odd = apply(sin_both, sin_high, imag) * scale
            later = even - odd
            earlier = even + odd
            for k in range(HALF + 1):
                out[r, HALF + k, a : a + 1, :] = later[k : k + 1]
            for k in range(1, HALF + 1):
                out[r, HALF - k, a : a + 1, :] = earlier[k : k + 1]


def on_device(spectra, match, counts):
    slots, parts, freq, block = spectra.shape
    chans = lax.axis_size("chan")
    bins = chans * lax.axis_size("seg")
    tile = slots * parts

    valid = (jnp.arange(slots, dtype=jnp.int32) < counts[0]).astype(jnp.bfloat16)
    own = spectra * valid[:, None, None, None]
    own = jnp.transpose(own, (2, 1, 0, 3)).reshape(freq, tile, block)
    ones = jnp.concatenate([valid, jnp.zeros_like(valid)])
    ones = jnp.broadcast_to(ones[None, :, None], (1, tile, block))
    rest = jnp.zeros((bins - freq - 1, tile, block), jnp.bfloat16)
    send = jnp.concatenate([own, ones, rest], axis=0)

    here = lax.all_to_all(send, ("chan", "seg"), 0, 0, tiled=True)
    here = here.reshape(chans, bins // chans * tile, block)

    rows = ROUNDS * tile
    cross = pl.pallas_call(
        cross_kernel,
        out_shape=jax.ShapeDtypeStruct((bins, rows, block), jnp.float32),
        in_specs=[
            pl.BlockSpec(memory_space=pltpu.SMEM),
            pl.BlockSpec(memory_space=pltpu.VMEM),
        ],
        out_specs=pl.BlockSpec(memory_space=pltpu.VMEM),
        scratch_shapes=[pltpu.VMEM((chans, 2 * block, 2 * block), jnp.bfloat16)],
        compiler_params=pltpu.CompilerParams(vmem_limit_bytes=24 * 1024 * 1024),
        name="cross",
    )(match, here)

    mine = lax.all_to_all(cross, ("chan", "seg"), 0, 0, tiled=True)
    mine = mine.reshape(bins * rows, block)

    cos, sin = tables(freq, bins)
    return pl.pallas_call(
        lambda *refs: lag_kernel(freq, *refs),
        out_shape=jax.ShapeDtypeStruct((ROUNDS, LAGS, tile // 2, block), jnp.float32),
        in_specs=[pl.BlockSpec(memory_space=pltpu.VMEM)] * 3,
        out_specs=pl.BlockSpec(memory_space=pltpu.VMEM),
        compiler_params=pltpu.CompilerParams(vmem_limit_bytes=24 * 1024 * 1024),
        name="lags",
    )(jnp.asarray(cos), jnp.asarray(sin), mine)


def solution(mesh):
    return jax.shard_map(
        on_device,
        mesh=mesh,
        in_specs=(P("seg", None, None, "chan"), P(), P("seg")),
        out_specs=P(None, None, ("chan", "seg"), None),
        check_vma=False,
    )
```

```python
import functools

import jax
import jax.numpy as jnp
import numpy as np
from jax import lax
from jax.experimental import pallas as pl
from jax.experimental.pallas import tpu as pltpu
from jax.sharding import PartitionSpec as P

LAGS = 51
SAMPLES = 3000
ROUNDS = 3
HALF = LAGS // 2
ROWS = 32
LANES = 128

KNEE = 2.0**-10
TOP = 32000.0
UNIT = 8192.0


def tables(freq, bins):
    lag = np.arange(ROWS, dtype=np.float64)[:, None]
    f = np.arange(bins, dtype=np.float64)[None, :] + 1.0
    angle = 2.0 * np.pi * f * lag / SAMPLES
    live = (np.arange(bins)[None, :] < freq) & (np.arange(ROWS)[:, None] <= HALF)
    return (
        np.where(live, np.cos(angle), 0.0).astype(np.float32),
        np.where(live, np.sin(angle), 0.0).astype(np.float32),
    )


def per_octave(depth):
    return TOP / float(np.log2(1.0 + depth / KNEE))


def send_kernel(counts, x, out, rows):
    slots, parts, freq, block = x.shape
    bins, tile, _ = out.shape
    rows[freq * tile :, :] = jnp.zeros(((bins - freq) * tile, block), jnp.float32)
    peak = jnp.zeros((freq, block), jnp.float32)
    for s in range(slots):
        valid = (s < counts[0]).astype(jnp.float32)
        for p in range(parts):
            at = p * slots + s
            v = x[s, p].astype(jnp.float32) * valid
            rows[pl.ds(at, freq, stride=tile), :] = v
            peak = jnp.maximum(peak, jnp.abs(v))
        rows[freq * tile + s : freq * tile + s + 1, :] = jnp.full((1, block), valid, jnp.float32)
    peak = jnp.concatenate([peak, jnp.zeros((2 * LANES - freq, block), jnp.float32)], axis=0)
    for i in range(2):
        row = (freq + 1) * tile + i
        part = jnp.transpose(peak[i * LANES : (i + 1) * LANES, :])
        rows[row : row + 1, :] = jnp.max(part, axis=0, keepdims=True)
    out[...] = rows[...].astype(jnp.bfloat16).reshape(out.shape)


def cross_kernel(freq, place, match, x, out, order, peak):
    blocks, depth, block = x.shape
    sources, rows, _ = out.shape
    tile = rows // ROUNDS
    half = tile // 2
    c = pl.program_id(0)

    @pl.when(c == 0)
    def _():
        row = lax.broadcasted_iota(jnp.int32, (2 * block, 2 * block), 0)
        col = lax.broadcasted_iota(jnp.int32, (2 * block, 2 * block), 1)
        channel = (row // tile) * half + row % half
        part = (row % tile) // half
        order[...] = (col == part * block + channel).astype(jnp.bfloat16)
        peak[0] = jnp.max(jnp.abs(x[...].astype(jnp.float32)))

    most = peak[0]
    inverse = jnp.where(most > 0.0, 1.0 / jnp.maximum(most, 1e-37), 0.0)

    own = x[c]
    groups = own.astype(jnp.float32).reshape(sources, tile, block)
    swapped = jnp.concatenate([groups[:, half:], -groups[:, :half]], axis=1)
    both = jnp.concatenate([own, swapped.reshape(depth, block).astype(jnp.bfloat16)], axis=1)
    turned = lax.dot_general(
        order[...], both, (((1,), (1,)), ((), ())), preferred_element_type=jnp.float32
    ).astype(jnp.bfloat16)
    coded = []
    for r in range(ROUNDS):
        product = jnp.dot(turned, x[match[r, c]], preferred_element_type=jnp.float32)
        y = product * inverse * inverse
        code = jnp.log2(1.0 + jnp.abs(y) * (1.0 / KNEE)) * per_octave(depth)
        code = jnp.round(jnp.where(y < 0.0, -code, code))
        coded.append(code.astype(jnp.int32).astype(jnp.int16).reshape(sources, tile, block))
    out[...] = jnp.concatenate(coded, axis=1)

    @pl.when(place[0] == freq + 1)
    def _():
        most = jnp.max(x[...].astype(jnp.float32).reshape(blocks * sources, tile, block), axis=0)
        power = jnp.floor(jnp.log2(jnp.maximum(most, 1e-37)))
        share = jnp.round(most * jnp.exp2(-power) * UNIT)
        rest = jnp.zeros(((ROUNDS - 2) * tile, block), jnp.float32)
        both = jnp.concatenate([power, share, rest], axis=0).astype(jnp.int32).astype(jnp.int16)
        out[...] = jnp.broadcast_to(both[None], out.shape)


def split(v):
    high = v.astype(jnp.bfloat16)
    return high, (v - high.astype(jnp.float32)).astype(jnp.bfloat16)


def lag_kernel(freq, depth, cos, sin, coded, out, x):
    bins = cos.shape[1]
    rows = coded.shape[1]
    tile = rows // ROUNDS
    half = tile // 2
    x[...] = coded[...].astype(jnp.int32).reshape(x.shape)

    at = (freq + 1) * rows
    power = x[at : at + tile, :].astype(jnp.float32)
    share = x[at + tile : at + 2 * tile, :].astype(jnp.float32)
    most = share * jnp.exp2(power) * (1.0 / UNIT)
    most = jnp.concatenate([most[i : i + 1] for i in range(bins // LANES)], axis=1)

    def both(table):
        high, low = split(table[...] * most * most * KNEE)
        return jnp.concatenate([high, low], axis=0), high

    def apply(tables, v):
        high, low = split(v)
        first = jnp.dot(tables[0], high, preferred_element_type=jnp.float32)
        return first[:ROWS] + first[ROWS:] + jnp.dot(tables[1], low, preferred_element_type=jnp.float32)

    def load(at):
        code = x[pl.ds(at, bins, stride=rows), :].astype(jnp.float32)
        size = jnp.exp2(jnp.abs(code) * (1.0 / per_octave(depth))) - 1.0
        return jnp.where(code < 0.0, -size, size)

    cos = both(cos)
    sin = both(sin)
    for r in range(ROUNDS):
        for a in range(half):
            real = load(r * tile + a)
            imag = load(r * tile + a + half)
            total = jnp.round(real[freq : freq + 1, :] * KNEE)
            scale = lax.rsqrt(total * jnp.float32(freq))
            even = apply(cos, real) * scale
            odd = apply(sin, imag) * scale
            later = even - odd
            earlier = even + odd
            for k in range(HALF + 1):
                out[r, HALF + k, a : a + 1, :] = later[k : k + 1]
            for k in range(1, HALF + 1):
                out[r, HALF - k, a : a + 1, :] = earlier[k : k + 1]


def on_device(spectra, match, counts):
    slots, parts, freq, block = spectra.shape
    chans = lax.axis_size("chan")
    segs = lax.axis_size("seg")
    bins = chans * segs
    tile = slots * parts
    depth = segs * tile
    rows = ROUNDS * tile
    place = lax.axis_index("chan") * segs + lax.axis_index("seg")

    vmem = pl.BlockSpec(memory_space=pltpu.VMEM)
    smem = pl.BlockSpec(memory_space=pltpu.SMEM)
    params = pltpu.CompilerParams(vmem_limit_bytes=24 * 1024 * 1024)

    send = pl.pallas_call(
        send_kernel,
        out_shape=jax.ShapeDtypeStruct((bins, tile, block), jnp.bfloat16),
        in_specs=[smem, vmem],
        out_specs=vmem,
        scratch_shapes=[pltpu.VMEM((bins * tile, block), jnp.float32)],
        compiler_params=params,
        name="send",
    )(counts, spectra)

    here = lax.all_to_all(send, ("chan", "seg"), 0, 0, tiled=True)
    here = here.reshape(chans, depth, block)

    cross = pl.pallas_call(
        functools.partial(cross_kernel, freq),
        grid=(chans,),
        out_shape=jax.ShapeDtypeStruct((bins, rows, block), jnp.int16),
        in_specs=[smem, smem, vmem],
        out_specs=pl.BlockSpec((segs, rows, block), lambda c: (c, 0, 0)),
        scratch_shapes=[
            pltpu.VMEM((2 * block, 2 * block), jnp.bfloat16),
            pltpu.SMEM((1,), jnp.float32),
        ],
        compiler_params=params,
        name="cross",
    )(place.astype(jnp.int32).reshape(1), match, here)

    mine = lax.all_to_all(cross, ("chan", "seg"), 0, 0, tiled=True)

    cos, sin = tables(freq, bins)
    return pl.pallas_call(
        functools.partial(lag_kernel, freq, depth),
        out_shape=jax.ShapeDtypeStruct((ROUNDS, LAGS, tile // 2, block), jnp.float32),
        in_specs=[vmem] * 3,
        out_specs=vmem,
        scratch_shapes=[pltpu.VMEM((bins * rows, block), jnp.int32)],
        compiler_params=params,
        name="lags",
    )(jnp.asarray(cos), jnp.asarray(sin), mine)


def solution(mesh):
    return jax.shard_map(
        on_device,
        mesh=mesh,
        in_specs=(P("seg", None, None, "chan"), P(), P("seg")),
        out_specs=P(None, None, ("chan", "seg"), None),
        check_vma=False,
    )
```

```python
import functools

import jax
import jax.numpy as jnp
import numpy as np
from jax import lax
from jax.experimental import pallas as pl
from jax.experimental.pallas import tpu as pltpu
from jax.sharding import PartitionSpec as P

LAGS = 51
SAMPLES = 3000
ROUNDS = 3
HALF = LAGS // 2
ROWS = 32
LANES = 128

KNEE = 2.0**-10
TOP = 32000.0
UNIT = 8192.0


def tables(freq, bins):
    lag = np.arange(ROWS, dtype=np.float64)[:, None]
    f = np.arange(bins, dtype=np.float64)[None, :] + 1.0
    angle = 2.0 * np.pi * f * lag / SAMPLES
    live = (np.arange(bins)[None, :] < freq) & (np.arange(ROWS)[:, None] <= HALF)
    return (
        np.where(live, np.cos(angle), 0.0).astype(np.float32),
        np.where(live, np.sin(angle), 0.0).astype(np.float32),
    )


def per_e(depth):
    return TOP / float(np.log(1.0 + depth / KNEE))


def send_kernel(counts, x, out, rows):
    slots, parts, freq, block = x.shape
    bins, tile, _ = out.shape
    rows[freq * tile :, :] = jnp.zeros(((bins - freq) * tile, block), jnp.float32)
    peak = jnp.zeros((freq, block), jnp.float32)
    for s in range(slots):
        valid = (s < counts[0]).astype(jnp.float32)
        for p in range(parts):
            at = p * slots + s
            v = x[s, p].astype(jnp.float32) * valid
            rows[pl.ds(at, freq, stride=tile), :] = v
            peak = jnp.maximum(peak, jnp.abs(v))
        rows[freq * tile + s : freq * tile + s + 1, :] = jnp.full((1, block), valid, jnp.float32)
    peak = jnp.concatenate([peak, jnp.zeros((2 * LANES - freq, block), jnp.float32)], axis=0)
    for i in range(2):
        row = (freq + 1) * tile + i
        part = jnp.transpose(peak[i * LANES : (i + 1) * LANES, :])
        rows[row : row + 1, :] = jnp.max(part, axis=0, keepdims=True)
    out[...] = rows[...].astype(jnp.bfloat16).reshape(out.shape)


def cross_kernel(freq, place, match, x, out):
    blocks, depth, block = x.shape
    bins, rows, _ = out.shape
    sources = bins // blocks
    tile = rows // ROUNDS
    half = tile // 2

    row = lax.broadcasted_iota(jnp.int32, (2 * block, 2 * block), 0)
    col = lax.broadcasted_iota(jnp.int32, (2 * block, 2 * block), 1)
    channel = (row // tile) * half + row % half
    part = (row % tile) // half
    order = (col == part * block + channel).astype(jnp.bfloat16)
    most = jnp.max(jnp.abs(x[...].astype(jnp.float32)))
    inverse = jnp.where(most > 0.0, 1.0 / jnp.maximum(most, 1e-37), 0.0)

    def one(c):
        own = x[c]
        groups = own.astype(jnp.float32).reshape(sources, tile, block)
        swapped = jnp.concatenate([groups[:, half:], -groups[:, :half]], axis=1)
        both = jnp.concatenate([own, swapped.reshape(depth, block).astype(jnp.bfloat16)], axis=1)
        turned = lax.dot_general(
            order, both, (((1,), (1,)), ((), ())), preferred_element_type=jnp.float32
        ).astype(jnp.bfloat16)
        coded = []
        for r in range(ROUNDS):
            product = jnp.dot(turned, x[match[r, c]], preferred_element_type=jnp.float32)
            y = product * (inverse * (1.0 / KNEE)) * inverse
            code = (jnp.log(1.0 + jnp.abs(y)) * per_e(depth) + 0.5).astype(jnp.int32)
            code = jnp.where(y < 0.0, -code, code)
            coded.append(code.astype(jnp.int16).reshape(sources, tile, block))
        out[pl.ds(c * sources, sources)] = jnp.concatenate(coded, axis=1)

    for c in range(blocks):
        one(c)

    @pl.when(place[0] == freq + 1)
    def _():
        most = jnp.max(x[...].astype(jnp.float32).reshape(blocks * sources, tile, block), axis=0)
        power = jnp.floor(jnp.log2(jnp.maximum(most, 1e-37)))
        share = jnp.round(most * jnp.exp2(-power) * UNIT)
        rest = jnp.zeros(((ROUNDS - 2) * tile, block), jnp.float32)
        both = jnp.concatenate([power, share, rest], axis=0).astype(jnp.int32).astype(jnp.int16)
        out[...] = jnp.broadcast_to(both[None], out.shape)


def split(v):
    high = v.astype(jnp.bfloat16)
    return high, (v - high.astype(jnp.float32)).astype(jnp.bfloat16)


def lag_kernel(freq, depth, cos, sin, coded, out, x):
    bins = cos.shape[1]
    rows = coded.shape[1]
    tile = rows // ROUNDS
    half = tile // 2
    x[...] = coded[...].astype(jnp.int32).reshape(x.shape)

    at = (freq + 1) * rows
    power = x[at : at + tile, :].astype(jnp.float32)
    share = x[at + tile : at + 2 * tile, :].astype(jnp.float32)
    most = share * jnp.exp2(power) * (1.0 / UNIT)
    most = jnp.concatenate([most[i : i + 1] for i in range(bins // LANES)], axis=1)

    def both(table):
        high, low = split(table[...] * most * most * KNEE)
        return jnp.concatenate([high, low], axis=0), high

    def apply(tables, v):
        high, low = split(v)
        first = jnp.dot(tables[0], high, preferred_element_type=jnp.float32)
        return first[:ROWS] + first[ROWS:] + jnp.dot(tables[1], low, preferred_element_type=jnp.float32)

    def load(at):
        code = x[pl.ds(at, bins, stride=rows), :].astype(jnp.float32)
        size = jnp.exp(jnp.abs(code) * (1.0 / per_e(depth))) - 1.0
        return jnp.where(code < 0.0, -size, size)

    cos = both(cos)
    sin = both(sin)
    for r in range(ROUNDS):
        for a in range(0, half, 2):
            real = jnp.concatenate([load(r * tile + a), load(r * tile + a + 1)], axis=1)
            imag = jnp.concatenate([load(r * tile + a + half), load(r * tile + a + 1 + half)], axis=1)
            total = jnp.round(real[freq : freq + 1, :] * KNEE)
            scale = lax.rsqrt(total * jnp.float32(freq))
            even = apply(cos, real) * scale
            odd = apply(sin, imag) * scale
            later = even - odd
            earlier = even + odd
            for i in range(2):
                at = slice(i * LANES, (i + 1) * LANES)
                for k in range(HALF + 1):
                    out[r, HALF + k, a + i : a + i + 1, :] = later[k : k + 1, at]
                for k in range(1, HALF + 1):
                    out[r, HALF - k, a + i : a + i + 1, :] = earlier[k : k + 1, at]


def kernels(slots, parts, freq, block, chans, segs):
    bins = chans * segs
    tile = slots * parts
    depth = segs * tile
    rows = ROUNDS * tile

    vmem = pl.BlockSpec(memory_space=pltpu.VMEM)
    smem = pl.BlockSpec(memory_space=pltpu.SMEM)
    params = pltpu.CompilerParams(vmem_limit_bytes=24 * 1024 * 1024)

    send = pl.pallas_call(
        send_kernel,
        out_shape=jax.ShapeDtypeStruct((bins, tile, block), jnp.bfloat16),
        in_specs=[smem, vmem],
        out_specs=vmem,
        scratch_shapes=[pltpu.VMEM((bins * tile, block), jnp.float32)],
        compiler_params=params,
        name="send",
    )
    cross = pl.pallas_call(
        functools.partial(cross_kernel, freq),
        out_shape=jax.ShapeDtypeStruct((bins, rows, block), jnp.int16),
        in_specs=[smem, smem, vmem],
        out_specs=vmem,
        compiler_params=params,
        name="cross",
    )
    lags = pl.pallas_call(
        functools.partial(lag_kernel, freq, depth),
        out_shape=jax.ShapeDtypeStruct((ROUNDS, LAGS, tile // 2, block), jnp.float32),
        in_specs=[vmem] * 3,
        out_specs=vmem,
        scratch_shapes=[pltpu.VMEM((bins * rows, block), jnp.int32)],
        compiler_params=params,
        name="lags",
    )
    cos, sin = tables(freq, bins)
    return send, cross, functools.partial(lags, jnp.asarray(cos), jnp.asarray(sin))


def on_device(spectra, match, counts):
    slots, parts, freq, block = spectra.shape
    chans = lax.axis_size("chan")
    segs = lax.axis_size("seg")
    place = lax.axis_index("chan") * segs + lax.axis_index("seg")
    send, cross, lags = kernels(slots, parts, freq, block, chans, segs)

    here = lax.all_to_all(send(counts, spectra), ("chan", "seg"), 0, 0, tiled=True)
    here = here.reshape(chans, segs * slots * parts, block)
    coded = cross(place.astype(jnp.int32).reshape(1), match, here)
    return lags(lax.all_to_all(coded, ("chan", "seg"), 0, 0, tiled=True))


def solution(mesh):
    return jax.shard_map(
        on_device,
        mesh=mesh,
        in_specs=(P("seg", None, None, "chan"), P(), P("seg")),
        out_specs=P(None, None, ("chan", "seg"), None),
        check_vma=False,
    )
```

```python
import functools

import jax
import jax.numpy as jnp
import numpy as np
from jax import lax
from jax.experimental import pallas as pl
from jax.experimental.pallas import tpu as pltpu
from jax.sharding import PartitionSpec as P

LAGS = 51
SAMPLES = 3000
ROUNDS = 3
HALF = LAGS // 2
ROWS = 32
LANES = 128

KNEE = 2.0**-16
TOP = 32000.0
UNIT = 8192.0


def tables(freq, bins):
    lag = np.arange(ROWS, dtype=np.float64)[:, None]
    f = np.arange(bins, dtype=np.float64)[None, :] + 1.0
    angle = 2.0 * np.pi * f * lag / SAMPLES
    live = (np.arange(bins)[None, :] < freq) & (np.arange(ROWS)[:, None] <= HALF)
    return (
        np.where(live, np.cos(angle), 0.0).astype(np.float32),
        np.where(live, np.sin(angle), 0.0).astype(np.float32),
    )


def per_e(depth):
    return TOP / float(np.log(1.0 + depth / KNEE))


def send_kernel(counts, x, out, rows):
    slots, parts, freq, block = x.shape
    bins, tile, _ = out.shape
    rows[freq * tile :, :] = jnp.zeros(((bins - freq) * tile, block), jnp.float32)
    peak = jnp.zeros((freq, block), jnp.float32)
    for s in range(slots):
        valid = (s < counts[0]).astype(jnp.float32)
        for p in range(parts):
            at = p * slots + s
            v = x[s, p].astype(jnp.float32) * valid
            rows[pl.ds(at, freq, stride=tile), :] = v
            peak = jnp.maximum(peak, jnp.abs(v))
        rows[freq * tile + s : freq * tile + s + 1, :] = jnp.full((1, block), valid, jnp.float32)
    peak = jnp.concatenate([peak, jnp.zeros((2 * LANES - freq, block), jnp.float32)], axis=0)
    for i in range(2):
        row = (freq + 1) * tile + i
        part = jnp.transpose(peak[i * LANES : (i + 1) * LANES, :])
        rows[row : row + 1, :] = jnp.max(part, axis=0, keepdims=True)
    out[...] = rows[...].astype(jnp.bfloat16).reshape(out.shape)


def cross_kernel(freq, place, match, x, out):
    blocks, depth, block = x.shape
    bins, rows, _ = out.shape
    sources = bins // blocks
    tile = rows // ROUNDS
    half = tile // 2

    row = lax.broadcasted_iota(jnp.int32, (2 * block, 2 * block), 0)
    col = lax.broadcasted_iota(jnp.int32, (2 * block, 2 * block), 1)
    channel = (row // tile) * half + row % half
    part = (row % tile) // half
    order = (col == part * block + channel).astype(jnp.bfloat16)
    most = jnp.max(jnp.abs(x[...].astype(jnp.float32)))
    inverse = jnp.where(most > 0.0, 1.0 / jnp.maximum(most, 1e-37), 0.0)

    def one(c):
        own = x[c]
        groups = own.astype(jnp.float32).reshape(sources, tile, block)
        swapped = jnp.concatenate([groups[:, half:], -groups[:, :half]], axis=1)
        both = jnp.concatenate([own, swapped.reshape(depth, block).astype(jnp.bfloat16)], axis=1)
        turned = lax.dot_general(
            order, both, (((1,), (1,)), ((), ())), preferred_element_type=jnp.float32
        ).astype(jnp.bfloat16)
        coded = []
        for r in range(ROUNDS):
            product = jnp.dot(turned, x[match[r, c]], preferred_element_type=jnp.float32)
            y = product * (inverse * (1.0 / KNEE)) * inverse
            code = (jnp.log(1.0 + jnp.abs(y)) * per_e(depth) + 0.5).astype(jnp.int32)
            code = jnp.where(y < 0.0, -code, code)
            coded.append(code.astype(jnp.int16).reshape(sources, tile, block))
        out[pl.ds(c * sources, sources)] = jnp.concatenate(coded, axis=1)

    for c in range(blocks):
        one(c)

    @pl.when(place[0] == freq + 1)
    def _():
        most = jnp.max(x[...].astype(jnp.float32).reshape(blocks * sources, tile, block), axis=0)
        power = jnp.floor(jnp.log2(jnp.maximum(most, 1e-37)))
        share = jnp.round(most * jnp.exp2(-power) * UNIT)
        rest = jnp.zeros(((ROUNDS - 2) * tile, block), jnp.float32)
        both = jnp.concatenate([power, share, rest], axis=0).astype(jnp.int32).astype(jnp.int16)
        out[...] = jnp.broadcast_to(both[None], out.shape)


def split(v):
    high = v.astype(jnp.bfloat16)
    return high, (v - high.astype(jnp.float32)).astype(jnp.bfloat16)


def lag_kernel(freq, depth, cos, sin, coded, out, x):
    bins = cos.shape[1]
    rows = coded.shape[1]
    tile = rows // ROUNDS
    half = tile // 2
    x[: bins * rows] = coded[...].astype(jnp.int32).reshape(bins * rows, LANES)

    at = (freq + 1) * rows
    power = x[at : at + tile, :].astype(jnp.float32)
    share = x[at + tile : at + 2 * tile, :].astype(jnp.float32)
    most = share * jnp.exp2(power) * (1.0 / UNIT)
    most = jnp.concatenate([most[i : i + 1] for i in range(bins // LANES)], axis=1)

    def both(table):
        high, low = split(table[...] * most * most * KNEE)
        return jnp.concatenate([high, low], axis=0), high

    def apply(tables, v):
        high, low = split(v)
        first = jnp.dot(tables[0], high, preferred_element_type=jnp.float32)
        return first[:ROWS] + first[ROWS:] + jnp.dot(tables[1], low, preferred_element_type=jnp.float32)

    def load(at):
        code = x[pl.ds(at, bins, stride=rows), :].astype(jnp.float32)
        size = jnp.exp(jnp.abs(code) * (1.0 / per_e(depth))) - 1.0
        return jnp.where(code < 0.0, -size, size)

    cos = both(cos)
    sin = both(sin)
    for r in range(ROUNDS):
        for a in range(0, half, 2):
            real = jnp.concatenate([load(r * tile + a), load(r * tile + a + 1)], axis=1)
            imag = jnp.concatenate([load(r * tile + a + half), load(r * tile + a + 1 + half)], axis=1)
            total = jnp.round(real[freq : freq + 1, :] * KNEE)
            scale = lax.rsqrt(total * jnp.float32(freq))
            even = apply(cos, real) * scale
            odd = apply(sin, imag) * scale
            later = even - odd
            earlier = even + odd
            for i in range(2):
                at = slice(i * LANES, (i + 1) * LANES)
                for k in range(HALF + 1):
                    out[r, HALF + k, a + i : a + i + 1, :] = later[k : k + 1, at]
                for k in range(1, HALF + 1):
                    out[r, HALF - k, a + i : a + i + 1, :] = earlier[k : k + 1, at]


def kernels(slots, parts, freq, block, chans, segs):
    bins = chans * segs
    tile = slots * parts
    depth = segs * tile
    rows = ROUNDS * tile

    vmem = pl.BlockSpec(memory_space=pltpu.VMEM)
    smem = pl.BlockSpec(memory_space=pltpu.SMEM)
    params = pltpu.CompilerParams(vmem_limit_bytes=24 * 1024 * 1024)

    send = pl.pallas_call(
        send_kernel,
        out_shape=jax.ShapeDtypeStruct((bins, tile, block), jnp.bfloat16),
        in_specs=[smem, vmem],
        out_specs=vmem,
        scratch_shapes=[pltpu.VMEM((bins * tile, block), jnp.float32)],
        compiler_params=params,
        name="send",
    )
    cross = pl.pallas_call(
        functools.partial(cross_kernel, freq),
        out_shape=jax.ShapeDtypeStruct((bins, rows, block), jnp.int16),
        in_specs=[smem, smem, vmem],
        out_specs=vmem,
        compiler_params=params,
        name="cross",
    )
    lags = pl.pallas_call(
        functools.partial(lag_kernel, freq, depth),
        out_shape=jax.ShapeDtypeStruct((ROUNDS, LAGS, tile // 2, block), jnp.float32),
        in_specs=[vmem] * 3,
        out_specs=vmem,
        scratch_shapes=[pltpu.VMEM(((bins + 1) * rows, block), jnp.int32)],
        compiler_params=params,
        name="lags",
    )
    cos, sin = tables(freq, bins)
    return send, cross, functools.partial(lags, jnp.asarray(cos), jnp.asarray(sin))


def on_device(spectra, match, counts):
    slots, parts, freq, block = spectra.shape
    chans = lax.axis_size("chan")
    segs = lax.axis_size("seg")
    place = lax.axis_index("chan") * segs + lax.axis_index("seg")
    send, cross, lags = kernels(slots, parts, freq, block, chans, segs)

    here = lax.all_to_all(send(counts, spectra), ("chan", "seg"), 0, 0, tiled=True)
    here = here.reshape(chans, segs * slots * parts, block)
    coded = cross(place.astype(jnp.int32).reshape(1), match, here)
    return lags(lax.all_to_all(coded, ("chan", "seg"), 0, 0, tiled=True))


def solution(mesh):
    return jax.shard_map(
        on_device,
        mesh=mesh,
        in_specs=(P("seg", None, None, "chan"), P(), P("seg")),
        out_specs=P(None, None, ("chan", "seg"), None),
        check_vma=False,
    )
```

```python
import functools

import jax
import jax.numpy as jnp
import numpy as np
from jax import lax
from jax.experimental import pallas as pl
from jax.experimental.pallas import tpu as pltpu
from jax.sharding import PartitionSpec as P

LAGS = 51
SAMPLES = 3000
ROUNDS = 3
HALF = LAGS // 2
ROWS = 32
LANES = 128

KNEE = 2.0**-16
TOP = 32000.0
UNIT = 8192.0


def tables(freq, bins):
    lag = np.arange(ROWS, dtype=np.float64)[:, None]
    f = np.arange(bins, dtype=np.float64)[None, :] + 1.0
    angle = 2.0 * np.pi * f * lag / SAMPLES
    live = (np.arange(bins)[None, :] < freq) & (np.arange(ROWS)[:, None] <= HALF)
    return (
        np.where(live, np.cos(angle), 0.0).astype(np.float32),
        np.where(live, np.sin(angle), 0.0).astype(np.float32),
    )


def ranks(chans, segs):
    outer = segs // 2
    inner = chans * segs // outer
    return [i + outer * j for i in range(outer) for j in range(inner)]


def per_e(depth):
    return TOP / float(np.log(1.0 + depth / KNEE))


def send_kernel(counts, x, out, rows):
    slots, parts, freq, block = x.shape
    bins, tile, _ = out.shape
    rows[freq * tile :, :] = jnp.zeros(((bins - freq) * tile, block), jnp.float32)
    peak = jnp.zeros((freq, block), jnp.float32)
    for s in range(slots):
        valid = (s < counts[0]).astype(jnp.float32)
        for p in range(parts):
            at = p * slots + s
            v = x[s, p].astype(jnp.float32) * valid
            rows[pl.ds(at, freq, stride=tile), :] = v
            peak = jnp.maximum(peak, jnp.abs(v))
        rows[freq * tile + s : freq * tile + s + 1, :] = jnp.full((1, block), valid, jnp.float32)
    peak = jnp.concatenate([peak, jnp.zeros((2 * LANES - freq, block), jnp.float32)], axis=0)
    for i in range(2):
        row = (freq + 1) * tile + i
        part = jnp.transpose(peak[i * LANES : (i + 1) * LANES, :])
        rows[row : row + 1, :] = jnp.max(part, axis=0, keepdims=True)
    out[...] = rows[...].astype(jnp.bfloat16).reshape(out.shape)


def cross_kernel(freq, order, place, match, received, out, x):
    blocks, depth, block = x.shape
    bins, rows, _ = out.shape
    sources = bins // blocks
    tile = rows // ROUNDS
    half = tile // 2
    at = {device: i for i, device in enumerate(order)}

    for c in range(blocks):
        own = [received[at[c * sources + i]].astype(jnp.float32) for i in range(sources)]
        x[c] = jnp.concatenate(own, axis=0).astype(jnp.bfloat16)

    row = lax.broadcasted_iota(jnp.int32, (2 * block, 2 * block), 0)
    col = lax.broadcasted_iota(jnp.int32, (2 * block, 2 * block), 1)
    channel = (row // tile) * half + row % half
    part = (row % tile) // half
    select = (col == part * block + channel).astype(jnp.bfloat16)
    most = jnp.max(jnp.abs(x[...].astype(jnp.float32)))
    inverse = jnp.where(most > 0.0, 1.0 / jnp.maximum(most, 1e-37), 0.0)

    def one(c):
        own = x[c]
        groups = own.astype(jnp.float32).reshape(sources, tile, block)
        swapped = jnp.concatenate([groups[:, half:], -groups[:, :half]], axis=1)
        both = jnp.concatenate([own, swapped.reshape(depth, block).astype(jnp.bfloat16)], axis=1)
        turned = lax.dot_general(
            select, both, (((1,), (1,)), ((), ())), preferred_element_type=jnp.float32
        ).astype(jnp.bfloat16)
        coded = []
        for r in range(ROUNDS):
            product = jnp.dot(turned, x[match[r, c]], preferred_element_type=jnp.float32)
            y = product * (inverse * (1.0 / KNEE)) * inverse
            code = (jnp.log(1.0 + jnp.abs(y)) * per_e(depth) + 0.5).astype(jnp.int32)
            code = jnp.where(y < 0.0, -code, code)
            coded.append(code.astype(jnp.int16).reshape(sources, tile, block))
        for i in range(sources):
            out[at[c * sources + i]] = jnp.concatenate([code[i] for code in coded], axis=0)

    for c in range(blocks):
        one(c)

    @pl.when(place[0] == order[freq + 1])
    def _():
        most = jnp.max(x[...].astype(jnp.float32).reshape(blocks * sources, tile, block), axis=0)
        power = jnp.floor(jnp.log2(jnp.maximum(most, 1e-37)))
        share = jnp.round(most * jnp.exp2(-power) * UNIT)
        rest = jnp.zeros(((ROUNDS - 2) * tile, block), jnp.float32)
        both = jnp.concatenate([power, share, rest], axis=0).astype(jnp.int32).astype(jnp.int16)
        out[...] = jnp.broadcast_to(both[None], out.shape)


def split(v):
    high = v.astype(jnp.bfloat16)
    return high, (v - high.astype(jnp.float32)).astype(jnp.bfloat16)


def lag_kernel(freq, depth, cos, sin, coded, out, x):
    bins = cos.shape[1]
    rows = coded.shape[1]
    tile = rows // ROUNDS
    half = tile // 2
    x[: bins * rows] = coded[...].astype(jnp.int32).reshape(bins * rows, LANES)

    at = (freq + 1) * rows
    power = x[at : at + tile, :].astype(jnp.float32)
    share = x[at + tile : at + 2 * tile, :].astype(jnp.float32)
    most = share * jnp.exp2(power) * (1.0 / UNIT)
    most = jnp.concatenate([most[i : i + 1] for i in range(bins // LANES)], axis=1)

    def both(table):
        high, low = split(table[...] * most * most * KNEE)
        return jnp.concatenate([high, low], axis=0), high

    def apply(tables, v):
        high, low = split(v)
        first = jnp.dot(tables[0], high, preferred_element_type=jnp.float32)
        return first[:ROWS] + first[ROWS:] + jnp.dot(tables[1], low, preferred_element_type=jnp.float32)

    def load(at):
        code = x[pl.ds(at, bins, stride=rows), :].astype(jnp.float32)
        size = jnp.exp(jnp.abs(code) * (1.0 / per_e(depth))) - 1.0
        return jnp.where(code < 0.0, -size, size)

    cos = both(cos)
    sin = both(sin)
    for r in range(ROUNDS):
        for a in range(0, half, 2):
            real = jnp.concatenate([load(r * tile + a), load(r * tile + a + 1)], axis=1)
            imag = jnp.concatenate([load(r * tile + a + half), load(r * tile + a + 1 + half)], axis=1)
            total = jnp.round(real[freq : freq + 1, :] * KNEE)
            scale = lax.rsqrt(total * jnp.float32(freq))
            even = apply(cos, real) * scale
            odd = apply(sin, imag) * scale
            later = even - odd
            earlier = even + odd
            for i in range(2):
                at = slice(i * LANES, (i + 1) * LANES)
                for k in range(HALF + 1):
                    out[r, HALF + k, a + i : a + i + 1, :] = later[k : k + 1, at]
                for k in range(1, HALF + 1):
                    out[r, HALF - k, a + i : a + i + 1, :] = earlier[k : k + 1, at]


def kernels(slots, parts, freq, block, chans, segs):
    bins = chans * segs
    tile = slots * parts
    depth = segs * tile
    rows = ROUNDS * tile

    vmem = pl.BlockSpec(memory_space=pltpu.VMEM)
    smem = pl.BlockSpec(memory_space=pltpu.SMEM)
    params = pltpu.CompilerParams(vmem_limit_bytes=24 * 1024 * 1024)

    send = pl.pallas_call(
        send_kernel,
        out_shape=jax.ShapeDtypeStruct((bins, tile, block), jnp.bfloat16),
        in_specs=[smem, vmem],
        out_specs=vmem,
        scratch_shapes=[pltpu.VMEM((bins * tile, block), jnp.float32)],
        compiler_params=params,
        name="send",
    )
    cross = pl.pallas_call(
        functools.partial(cross_kernel, freq, ranks(chans, segs)),
        out_shape=jax.ShapeDtypeStruct((bins, rows, block), jnp.int16),
        in_specs=[smem, smem, vmem],
        out_specs=vmem,
        scratch_shapes=[pltpu.VMEM((chans, depth, block), jnp.bfloat16)],
        compiler_params=params,
        name="cross",
    )
    lags = pl.pallas_call(
        functools.partial(lag_kernel, freq, depth),
        out_shape=jax.ShapeDtypeStruct((ROUNDS, LAGS, tile // 2, block), jnp.float32),
        in_specs=[vmem] * 3,
        out_specs=vmem,
        scratch_shapes=[pltpu.VMEM(((bins + 1) * rows, block), jnp.int32)],
        compiler_params=params,
        name="lags",
    )
    cos, sin = tables(freq, bins)
    return send, cross, functools.partial(lags, jnp.asarray(cos), jnp.asarray(sin))


def on_device(spectra, match, counts):
    slots, parts, freq, block = spectra.shape
    chans = lax.axis_size("chan")
    segs = lax.axis_size("seg")
    place = lax.axis_index("chan") * segs + lax.axis_index("seg")
    groups = [ranks(chans, segs)]
    send, cross, lags = kernels(slots, parts, freq, block, chans, segs)

    here = lax.all_to_all(send(counts, spectra), ("chan", "seg"), 0, 0, axis_index_groups=groups, tiled=True)
    coded = cross(place.astype(jnp.int32).reshape(1), match, here)
    return lags(lax.all_to_all(coded, ("chan", "seg"), 0, 0, axis_index_groups=groups, tiled=True))


def solution(mesh):
    return jax.shard_map(
        on_device,
        mesh=mesh,
        in_specs=(P("seg", None, None, "chan"), P(), P("seg")),
        out_specs=P(None, None, ("chan", "seg"), None),
        check_vma=False,
    )
```

```python
import functools

import jax
import jax.numpy as jnp
import numpy as np
from jax import lax
from jax.experimental import pallas as pl
from jax.experimental.pallas import tpu as pltpu
from jax.sharding import PartitionSpec as P

LAGS = 51
SAMPLES = 3000
ROUNDS = 3
HALF = LAGS // 2
ROWS = 32
LANES = 128

KNEE = 2.0**-16
TOP = 32000.0
UNIT = 8192.0


def tables(freq, bins):
    lag = np.arange(ROWS, dtype=np.float64)[:, None]
    f = np.arange(bins, dtype=np.float64)[None, :] + 1.0
    angle = 2.0 * np.pi * f * lag / SAMPLES
    live = (np.arange(bins)[None, :] < freq) & (np.arange(ROWS)[:, None] <= HALF)
    return (
        np.where(live, np.cos(angle), 0.0).astype(np.float32),
        np.where(live, np.sin(angle), 0.0).astype(np.float32),
    )


def ranks(chans, segs):
    low = segs // 2

    def key(device):
        chan, seg = device // segs, device % segs
        return chan // 2 % 2, chan % 2, chan // 4, seg % low, seg // low

    return sorted(range(chans * segs), key=key)


def per_e(depth):
    return TOP / float(np.log(1.0 + depth / KNEE))


def send_kernel(counts, x, out, rows):
    slots, parts, freq, block = x.shape
    bins, tile, _ = out.shape
    rows[freq * tile :, :] = jnp.zeros(((bins - freq) * tile, block), jnp.float32)
    peak = jnp.zeros((freq, block), jnp.float32)
    for s in range(slots):
        valid = (s < counts[0]).astype(jnp.float32)
        for p in range(parts):
            at = p * slots + s
            v = x[s, p].astype(jnp.float32) * valid
            rows[pl.ds(at, freq, stride=tile), :] = v
            peak = jnp.maximum(peak, jnp.abs(v))
        rows[freq * tile + s : freq * tile + s + 1, :] = jnp.full((1, block), valid, jnp.float32)
    peak = jnp.concatenate([peak, jnp.zeros((2 * LANES - freq, block), jnp.float32)], axis=0)
    for i in range(2):
        row = (freq + 1) * tile + i
        part = jnp.transpose(peak[i * LANES : (i + 1) * LANES, :])
        rows[row : row + 1, :] = jnp.max(part, axis=0, keepdims=True)
    out[...] = rows[...].astype(jnp.bfloat16).reshape(out.shape)


def cross_kernel(freq, order, place, match, received, out, x):
    blocks, depth, block = x.shape
    bins, rows, _ = out.shape
    sources = bins // blocks
    tile = rows // ROUNDS
    half = tile // 2
    at = {device: i for i, device in enumerate(order)}

    for c in range(blocks):
        own = [received[at[c * sources + i]].astype(jnp.float32) for i in range(sources)]
        x[c] = jnp.concatenate(own, axis=0).astype(jnp.bfloat16)

    row = lax.broadcasted_iota(jnp.int32, (2 * block, 2 * block), 0)
    col = lax.broadcasted_iota(jnp.int32, (2 * block, 2 * block), 1)
    channel = (row // tile) * half + row % half
    part = (row % tile) // half
    select = (col == part * block + channel).astype(jnp.bfloat16)
    most = jnp.max(jnp.abs(x[...].astype(jnp.float32)))
    inverse = jnp.where(most > 0.0, 1.0 / jnp.maximum(most, 1e-37), 0.0)

    def one(c):
        own = x[c]
        groups = own.astype(jnp.float32).reshape(sources, tile, block)
        swapped = jnp.concatenate([groups[:, half:], -groups[:, :half]], axis=1)
        both = jnp.concatenate([own, swapped.reshape(depth, block).astype(jnp.bfloat16)], axis=1)
        turned = lax.dot_general(
            select, both, (((1,), (1,)), ((), ())), preferred_element_type=jnp.float32
        ).astype(jnp.bfloat16)
        coded = []
        for r in range(ROUNDS):
            product = jnp.dot(turned, x[match[r, c]], preferred_element_type=jnp.float32)
            y = product * (inverse * (1.0 / KNEE)) * inverse
            code = (jnp.log(1.0 + jnp.abs(y)) * per_e(depth) + 0.5).astype(jnp.int32)
            code = jnp.where(y < 0.0, -code, code)
            coded.append(code.astype(jnp.int16).reshape(sources, tile, block))
        for i in range(sources):
            out[at[c * sources + i]] = jnp.concatenate([code[i] for code in coded], axis=0)

    for c in range(blocks):
        one(c)

    @pl.when(place[0] == order[freq + 1])
    def _():
        most = jnp.max(x[...].astype(jnp.float32).reshape(blocks * sources, tile, block), axis=0)
        power = jnp.floor(jnp.log2(jnp.maximum(most, 1e-37)))
        share = jnp.round(most * jnp.exp2(-power) * UNIT)
        rest = jnp.zeros(((ROUNDS - 2) * tile, block), jnp.float32)
        both = jnp.concatenate([power, share, rest], axis=0).astype(jnp.int32).astype(jnp.int16)
        out[...] = jnp.broadcast_to(both[None], out.shape)


def split(v):
    high = v.astype(jnp.bfloat16)
    return high, (v - high.astype(jnp.float32)).astype(jnp.bfloat16)


def lag_kernel(freq, depth, cos, sin, coded, out, x):
    bins = cos.shape[1]
    rows = coded.shape[1]
    tile = rows // ROUNDS
    half = tile // 2
    x[: bins * rows] = coded[:bins].astype(jnp.int32).reshape(bins * rows, LANES)

    at = (freq + 1) * rows
    power = x[at : at + tile, :].astype(jnp.float32)
    share = x[at + tile : at + 2 * tile, :].astype(jnp.float32)
    most = share * jnp.exp2(power) * (1.0 / UNIT)
    most = jnp.concatenate([most[:1], most[1:2]], axis=1)[:, :bins]

    def both(table):
        high, low = split(table[...] * most * most * KNEE)
        return jnp.concatenate([high, low], axis=0), high

    def apply(tables, v):
        high, low = split(v)
        first = jnp.dot(tables[0], high, preferred_element_type=jnp.float32)
        return first[:ROWS] + first[ROWS:] + jnp.dot(tables[1], low, preferred_element_type=jnp.float32)

    def load(at):
        code = x[pl.ds(at, bins, stride=rows), :].astype(jnp.float32)
        size = jnp.exp(jnp.abs(code) * (1.0 / per_e(depth))) - 1.0
        return jnp.where(code < 0.0, -size, size)

    cos = both(cos)
    sin = both(sin)
    for r in range(ROUNDS):
        for a in range(0, half, 2):
            real = jnp.concatenate([load(r * tile + a), load(r * tile + a + 1)], axis=1)
            imag = jnp.concatenate([load(r * tile + a + half), load(r * tile + a + 1 + half)], axis=1)
            total = jnp.round(real[freq : freq + 1, :] * KNEE)
            scale = lax.rsqrt(total * jnp.float32(freq))
            even = apply(cos, real) * scale
            odd = apply(sin, imag) * scale
            later = even - odd
            earlier = even + odd
            for i in range(2):
                at = slice(i * LANES, (i + 1) * LANES)
                for k in range(HALF + 1):
                    out[r, HALF + k, a + i : a + i + 1, :] = later[k : k + 1, at]
                for k in range(1, HALF + 1):
                    out[r, HALF - k, a + i : a + i + 1, :] = earlier[k : k + 1, at]


def kernels(slots, parts, freq, block, chans, segs):
    bins = chans * segs
    tile = slots * parts
    depth = segs * tile
    rows = ROUNDS * tile
    used = min(bins, (freq + 2 + 15) // 16 * 16)

    vmem = pl.BlockSpec(memory_space=pltpu.VMEM)
    smem = pl.BlockSpec(memory_space=pltpu.SMEM)
    params = pltpu.CompilerParams(vmem_limit_bytes=24 * 1024 * 1024)

    send = pl.pallas_call(
        send_kernel,
        out_shape=jax.ShapeDtypeStruct((bins, tile, block), jnp.bfloat16),
        in_specs=[smem, vmem],
        out_specs=vmem,
        scratch_shapes=[pltpu.VMEM((bins * tile, block), jnp.float32)],
        compiler_params=params,
        name="send",
    )
    cross = pl.pallas_call(
        functools.partial(cross_kernel, freq, ranks(chans, segs)),
        out_shape=jax.ShapeDtypeStruct((bins, rows, block), jnp.int16),
        in_specs=[smem, smem, vmem],
        out_specs=vmem,
        scratch_shapes=[pltpu.VMEM((chans, depth, block), jnp.bfloat16)],
        compiler_params=params,
        name="cross",
    )
    lags = pl.pallas_call(
        functools.partial(lag_kernel, freq, depth),
        out_shape=jax.ShapeDtypeStruct((ROUNDS, LAGS, tile // 2, block), jnp.float32),
        in_specs=[vmem] * 3,
        out_specs=vmem,
        scratch_shapes=[pltpu.VMEM(((used + 1) * rows, block), jnp.int32)],
        compiler_params=params,
        name="lags",
    )
    cos, sin = tables(freq, used)
    return send, cross, functools.partial(lags, jnp.asarray(cos), jnp.asarray(sin))


def on_device(spectra, match, counts):
    slots, parts, freq, block = spectra.shape
    chans = lax.axis_size("chan")
    segs = lax.axis_size("seg")
    place = lax.axis_index("chan") * segs + lax.axis_index("seg")
    groups = [ranks(chans, segs)]
    send, cross, lags = kernels(slots, parts, freq, block, chans, segs)

    here = lax.all_to_all(send(counts, spectra), ("chan", "seg"), 0, 0, axis_index_groups=groups, tiled=True)
    coded = cross(place.astype(jnp.int32).reshape(1), match, here)
    return lags(lax.all_to_all(coded, ("chan", "seg"), 0, 0, axis_index_groups=groups, tiled=True))


def solution(mesh):
    return jax.shard_map(
        on_device,
        mesh=mesh,
        in_specs=(P("seg", None, None, "chan"), P(), P("seg")),
        out_specs=P(None, None, ("chan", "seg"), None),
        check_vma=False,
    )
```

```python
import functools

import jax
import jax.numpy as jnp
import numpy as np
from jax import lax
from jax.experimental import pallas as pl
from jax.experimental.pallas import tpu as pltpu
from jax.sharding import PartitionSpec as P

LAGS = 51
SAMPLES = 3000
ROUNDS = 3
HALF = LAGS // 2
ROWS = 32
LANES = 128

KNEE = 2.0**-16
TOP = 32000.0
UNIT = 8192.0


def tables(freq, bins):
    lag = np.arange(ROWS, dtype=np.float64)[:, None]
    f = np.arange(bins, dtype=np.float64)[None, :] + 1.0
    angle = 2.0 * np.pi * f * lag / SAMPLES
    live = (np.arange(bins)[None, :] < freq) & (np.arange(ROWS)[:, None] <= HALF)
    return (
        np.where(live, np.cos(angle), 0.0).astype(np.float32),
        np.where(live, np.sin(angle), 0.0).astype(np.float32),
    )


def ranks(chans, segs):
    low = segs // 2

    def key(device):
        chan, seg = device // segs, device % segs
        return chan // 2 % 2, chan % 2, chan // 4, seg % low, seg // low

    return sorted(range(chans * segs), key=key)


def per_e(depth):
    return TOP / float(np.log(1.0 + depth / KNEE))


def send_kernel(counts, x, out, rows):
    slots, parts, freq, block = x.shape
    bins, tile, _ = out.shape
    rows[freq * tile :, :] = jnp.zeros(((bins - freq) * tile, block), jnp.float32)
    peak = jnp.zeros((freq, block), jnp.float32)
    for s in range(slots):
        valid = (s < counts[0]).astype(jnp.float32)
        for p in range(parts):
            at = p * slots + s
            v = x[s, p].astype(jnp.float32) * valid
            rows[pl.ds(at, freq, stride=tile), :] = v
            peak = jnp.maximum(peak, jnp.abs(v))
        rows[freq * tile + s : freq * tile + s + 1, :] = jnp.full((1, block), valid, jnp.float32)
    peak = jnp.concatenate([peak, jnp.zeros((2 * LANES - freq, block), jnp.float32)], axis=0)
    for i in range(2):
        row = (freq + 1) * tile + i
        part = jnp.transpose(peak[i * LANES : (i + 1) * LANES, :])
        rows[row : row + 1, :] = jnp.max(part, axis=0, keepdims=True)
    out[...] = rows[...].astype(jnp.bfloat16).reshape(out.shape)


def cross_kernel(freq, order, place, match, received, out, x):
    blocks, depth, block = x.shape
    bins, rows, _ = out.shape
    sources = bins // blocks
    tile = rows // ROUNDS
    half = tile // 2
    at = {device: i for i, device in enumerate(order)}

    for c in range(blocks):
        own = [received[at[c * sources + i]].astype(jnp.float32) for i in range(sources)]
        x[c] = jnp.concatenate(own, axis=0).astype(jnp.bfloat16)

    row = lax.broadcasted_iota(jnp.int32, (2 * block, 2 * block), 0)
    col = lax.broadcasted_iota(jnp.int32, (2 * block, 2 * block), 1)
    channel = (row // tile) * half + row % half
    part = (row % tile) // half
    select = (col == part * block + channel).astype(jnp.bfloat16)
    most = jnp.max(jnp.abs(x[...].astype(jnp.float32)))
    inverse = jnp.where(most > 0.0, 1.0 / jnp.maximum(most, 1e-37), 0.0)

    def one(c):
        own = x[c]
        groups = own.astype(jnp.float32).reshape(sources, tile, block)
        swapped = jnp.concatenate([groups[:, half:], -groups[:, :half]], axis=1)
        both = jnp.concatenate([own, swapped.reshape(depth, block).astype(jnp.bfloat16)], axis=1)
        turned = lax.dot_general(
            select, both, (((1,), (1,)), ((), ())), preferred_element_type=jnp.float32
        ).astype(jnp.bfloat16)
        coded = []
        for r in range(ROUNDS):
            product = jnp.dot(turned, x[match[r, c]], preferred_element_type=jnp.float32)
            y = product * (inverse * (1.0 / KNEE)) * inverse
            code = (jnp.log(1.0 + jnp.abs(y)) * per_e(depth) + 0.5).astype(jnp.int32)
            code = jnp.where(y < 0.0, -code, code)
            coded.append(code.astype(jnp.int16).reshape(sources, tile, block))
        for i in range(sources):
            out[at[c * sources + i]] = jnp.concatenate([code[i] for code in coded], axis=0)

    for c in range(blocks):
        one(c)

    @pl.when(place[0] == order[freq + 1])
    def _():
        most = jnp.max(x[...].astype(jnp.float32).reshape(blocks * sources, tile, block), axis=0)
        power = jnp.floor(jnp.log2(jnp.maximum(most, 1e-37)))
        share = jnp.round(most * jnp.exp2(-power) * UNIT)
        rest = jnp.zeros(((ROUNDS - 2) * tile, block), jnp.float32)
        both = jnp.concatenate([power, share, rest], axis=0).astype(jnp.int32).astype(jnp.int16)
        out[...] = jnp.broadcast_to(both[None], out.shape)


def split(v):
    high = v.astype(jnp.bfloat16)
    return high, (v - high.astype(jnp.float32)).astype(jnp.bfloat16)


def lag_kernel(freq, depth, cos, sin, coded, out, x):
    bins = cos.shape[1]
    rows = coded.shape[1]
    tile = rows // ROUNDS
    half = tile // 2
    pitch = rows + 1
    groups = coded[:bins].reshape(bins // 8, 8, rows, LANES)
    for i in range(8):
        x[: bins // 8, i * pitch : i * pitch + rows, :] = groups[:, i].astype(jnp.int32)
    x = x.reshape((bins // 8 + 1) * 8 * pitch, LANES)

    at = (freq + 1) * pitch
    power = x[at : at + tile, :].astype(jnp.float32)
    share = x[at + tile : at + 2 * tile, :].astype(jnp.float32)
    most = share * jnp.exp2(power) * (1.0 / UNIT)
    most = jnp.concatenate([most[:1], most[1:2]], axis=1)[:, :bins]

    def both(table):
        high, low = split(table[...] * most * most * KNEE)
        return jnp.concatenate([high, low], axis=0), high

    def apply(tables, v):
        high, low = split(v)
        first = jnp.dot(tables[0], high, preferred_element_type=jnp.float32)
        return first[:ROWS] + first[ROWS:] + jnp.dot(tables[1], low, preferred_element_type=jnp.float32)

    def load(at):
        code = x[pl.ds(at, bins, stride=pitch), :].astype(jnp.float32)
        size = jnp.exp(jnp.abs(code) * (1.0 / per_e(depth))) - 1.0
        return jnp.where(code < 0.0, -size, size)

    cos = both(cos)
    sin = both(sin)
    for r in range(ROUNDS):
        for a in range(0, half, 2):
            real = jnp.concatenate([load(r * tile + a), load(r * tile + a + 1)], axis=1)
            imag = jnp.concatenate([load(r * tile + a + half), load(r * tile + a + 1 + half)], axis=1)
            total = jnp.round(real[freq : freq + 1, :] * KNEE)
            scale = lax.rsqrt(total * jnp.float32(freq))
            even = apply(cos, real) * scale
            odd = apply(sin, imag) * scale
            later = even - odd
            earlier = even + odd
            for i in range(2):
                at = slice(i * LANES, (i + 1) * LANES)
                for k in range(HALF + 1):
                    out[r, HALF + k, a + i : a + i + 1, :] = later[k : k + 1, at]
                for k in range(1, HALF + 1):
                    out[r, HALF - k, a + i : a + i + 1, :] = earlier[k : k + 1, at]


def kernels(slots, parts, freq, block, chans, segs):
    bins = chans * segs
    tile = slots * parts
    depth = segs * tile
    rows = ROUNDS * tile
    used = min(bins, (freq + 2 + 15) // 16 * 16)

    vmem = pl.BlockSpec(memory_space=pltpu.VMEM)
    smem = pl.BlockSpec(memory_space=pltpu.SMEM)
    params = pltpu.CompilerParams(vmem_limit_bytes=24 * 1024 * 1024)

    send = pl.pallas_call(
        send_kernel,
        out_shape=jax.ShapeDtypeStruct((bins, tile, block), jnp.bfloat16),
        in_specs=[smem, vmem],
        out_specs=vmem,
        scratch_shapes=[pltpu.VMEM((bins * tile, block), jnp.float32)],
        compiler_params=params,
        name="send",
    )
    cross = pl.pallas_call(
        functools.partial(cross_kernel, freq, ranks(chans, segs)),
        out_shape=jax.ShapeDtypeStruct((bins, rows, block), jnp.int16),
        in_specs=[smem, smem, vmem],
        out_specs=vmem,
        scratch_shapes=[pltpu.VMEM((chans, depth, block), jnp.bfloat16)],
        compiler_params=params,
        name="cross",
    )
    lags = pl.pallas_call(
        functools.partial(lag_kernel, freq, depth),
        out_shape=jax.ShapeDtypeStruct((ROUNDS, LAGS, tile // 2, block), jnp.float32),
        in_specs=[vmem] * 3,
        out_specs=vmem,
        scratch_shapes=[pltpu.VMEM((used // 8 + 1, 8 * (rows + 1), block), jnp.int32)],
        compiler_params=params,
        name="lags",
    )
    cos, sin = tables(freq, used)
    return send, cross, functools.partial(lags, jnp.asarray(cos), jnp.asarray(sin))


def on_device(spectra, match, counts):
    slots, parts, freq, block = spectra.shape
    chans = lax.axis_size("chan")
    segs = lax.axis_size("seg")
    place = lax.axis_index("chan") * segs + lax.axis_index("seg")
    groups = [ranks(chans, segs)]
    send, cross, lags = kernels(slots, parts, freq, block, chans, segs)

    here = lax.all_to_all(send(counts, spectra), ("chan", "seg"), 0, 0, axis_index_groups=groups, tiled=True)
    coded = cross(place.astype(jnp.int32).reshape(1), match, here)
    return lags(lax.all_to_all(coded, ("chan", "seg"), 0, 0, axis_index_groups=groups, tiled=True))


def solution(mesh):
    return jax.shard_map(
        on_device,
        mesh=mesh,
        in_specs=(P("seg", None, None, "chan"), P(), P("seg")),
        out_specs=P(None, None, ("chan", "seg"), None),
        check_vma=False,
    )
```
